32 devices in a mesh: ctx: 8 (over y, x, core), kv: 4 (over z).
Axes of the slice: x: 2, y: 2, z: 4, core: 2. Of those that a mesh axis runs over, the one named last changes fastest.
Arguments:
- queries: bfloat16 [4096, 32, 128], P('ctx', 'kv'), may hold values from -5 to 5
- key_heads: bfloat16 [4096, 4, 128], P('ctx', 'kv'), may hold values from -5 to 5
- value_head_rows: bfloat16 [4096, 4, 128], P('ctx', 'kv'), may hold values from -6 to 6
- out_grad: bfloat16 [4096, 32, 128], P('ctx', 'kv'), may hold values from -96 to 96
- doc_start: int32 [4096], P(('ctx', 'kv')), may hold values from 0 to 4095, as said below
Outputs:
- query_grad: bfloat16 [4096, 32, 128], P('ctx', 'kv')
- key_grad: bfloat16 [4096, 4, 128], P('ctx', 'kv')
- value_grad: bfloat16 [4096, 4, 128], P('ctx', 'kv')
The draws below stay inside these ranges and needn't reach their ends.
Inputs may be any that keep to these rules, and one draw needn't show every extreme that they name: doc_start[p] is the first position of the document holding p: doc_start[p] <= p, and doc_start[p] equals p or doc_start[p - 1]; the last position starts a document of its own.
All inputs are finite; a program needn't handle non-finite values.
Results may differ from the reference program's by a relative error of at most 0.04.
Values may be sent and summed in bfloat16 or wider, within the bound.
A program may use at most 192 MiB of HBM per device.

```python
import math
import jax
import jax.numpy as jnp
from jax import lax

HEAD_SIZE = 128
KEY_VALUE_HEADS = 4
HQ = 32
SPAN = 4
TOK_DEV = 512
PACKED_TOKENS = 4096


def draw_queries(key, part):
    key = jax.random.fold_in(key, 1)
    window_start = jnp.clip(jax.random.normal(key, (PACKED_TOKENS, HQ, HEAD_SIZE), jnp.float32), -4.5, 4.5)
    return window_start.astype(jnp.bfloat16)


def draw_key_heads(key, part):
    key = jax.random.fold_in(key, 2)
    window_start = jnp.clip(jax.random.normal(key, (PACKED_TOKENS, KEY_VALUE_HEADS, HEAD_SIZE), jnp.float32), -4.5, 4.5)
    return window_start.astype(jnp.bfloat16)


def draw_doc_start(key, part):
    key = jax.random.fold_in(key, 3)
    lengths = jax.random.randint(key, (PACKED_TOKENS,), TOK_DEV // 4, 2 * SPAN * TOK_DEV)
    ends = jnp.minimum(jnp.cumsum(lengths), PACKED_TOKENS)
    marks = jnp.zeros((PACKED_TOKENS + 1,), jnp.int32).at[ends].set(1)[:PACKED_TOKENS].at[0].set(1).at[PACKED_TOKENS - 1].set(1)
    places = jnp.arange(PACKED_TOKENS, dtype=jnp.int32)
    return lax.cummax(places * marks, axis=0)


def block_levels(key, shape, cuts, smallest, high):
    gain, own = 1.0, jax.random.fold_in(key, 6)
    for position, shards_of in cuts:
        draws = jnp.exp(jax.random.uniform(jax.random.fold_in(own, position), (shards_of,), jnp.float32, smallest / len(cuts), high / len(cuts)))
        gain = gain * jnp.repeat(draws, shape[position] // shards_of).reshape([-1 if axis == position else 1 for axis in range(len(shape))])
    return gain


def bell_draw(key, dims, width, bound, split=(), kind=jnp.bfloat16):
    level = block_levels(key, dims, split, -0.22, 0.18) if split else 1.0
    entries = jax.random.normal(key, dims, jnp.float32) * width * level
    return jnp.minimum(jnp.maximum(entries, -bound), bound).astype(kind)


def setup_inputs(seed: int = 0) -> dict:
    splits = jax.random.split(jax.random.key(seed), 6)
    return {
        "queries": draw_queries(jax.random.fold_in(splits[5], 71), 0),
        "key_heads": draw_key_heads(jax.random.fold_in(splits[5], 71), 0),
        "value_head_rows": bell_draw(splits[2], (PACKED_TOKENS, KEY_VALUE_HEADS, HEAD_SIZE), 1.0, 6.0, ((0, 8), (1, 4))),
        "out_grad": bell_draw(splits[3], (PACKED_TOKENS, HQ, HEAD_SIZE), 16.0, 96.0, ((0, 8), (1, 4))),
        "doc_start": draw_doc_start(jax.random.fold_in(splits[5], 71), 0),
    }


fill_value = -1e+30

def round_keep(values):
    return lax.optimization_barrier(values.astype(jnp.bfloat16)).astype(jnp.float32)

def reference(queries, key_heads, value_head_rows, out_grad, doc_start):
    token_count, head_count, head_width = queries.shape
    group_count = key_heads.shape[1]
    per_group = head_count // group_count
    block_len = TOK_DEV
    window = SPAN * block_len
    lead_rows = (SPAN - 1) * block_len
    logit_scale = 1.0 / math.sqrt(head_width)
    lead = jnp.zeros((lead_rows, group_count, head_width), key_heads.dtype)
    keys_padded = jnp.concatenate([lead, key_heads], 0)
    values_padded = jnp.concatenate([lead, value_head_rows], 0)

    def visit_block(carried, block_index):
        key_acc, value_acc = carried
        start = (block_index * block_len).astype(jnp.int32)
        query_block = lax.dynamic_slice_in_dim(queries, start, block_len, 0).reshape(block_len, group_count, per_group, head_width).astype(jnp.float32)
        gradient_block = lax.dynamic_slice_in_dim(out_grad, start, block_len, 0).reshape(block_len, group_count, per_group, head_width).astype(jnp.float32)
        bounds = lax.dynamic_slice_in_dim(doc_start, start, block_len, 0)
        key_window = lax.dynamic_slice_in_dim(keys_padded, start, window, 0).astype(jnp.float32)
        value_window = lax.dynamic_slice_in_dim(values_padded, start, window, 0).astype(jnp.float32)
        query_pos = start + jnp.arange(block_len, dtype=jnp.int32)
        key_pos = start - lead_rows + jnp.arange(window, dtype=jnp.int32)
        allowed = (key_pos[None, :] <= query_pos[:, None]) & (key_pos[None, :] >= bounds[:, None])
        raw_scores = jnp.einsum('mpeb,hpb->pemh', query_block, key_window) * logit_scale
        scores = jnp.where(allowed[None, None], raw_scores, fill_value)
        row_max = lax.optimization_barrier(jnp.max(scores, -1))
        unscaled = jnp.where(allowed[None, None], jnp.exp(scores - row_max[..., None]), 0.0)
        totals = lax.optimization_barrier(jnp.sum(unscaled, -1))
        softmax_weights = round_keep(unscaled)
        summed_rows = jnp.einsum('fjqw,wfk->qfjk', softmax_weights, value_window)
        attn_out = (summed_rows / jnp.transpose(totals, (2, 0, 1))[..., None]).astype(jnp.bfloat16)
        row_dot = lax.optimization_barrier(jnp.sum(gradient_block * attn_out.astype(jnp.float32), -1))
        attn_prob = unscaled / totals[..., None]
        probability_block = round_keep(attn_prob)
        value_portion = jnp.einsum('qnjo,jqnu->oqu', probability_block, gradient_block)
        probability_gradient = jnp.einsum('mpeb,hpb->pemh', gradient_block, value_window)
        score_gradient = round_keep(attn_prob * (probability_gradient - jnp.transpose(row_dot, (1, 2, 0))[..., None]) * logit_scale)
        query_portion = jnp.einsum('fjqw,wfk->qfjk', score_gradient, key_window)
        key_portion = jnp.einsum('qnjo,jqnu->oqu', score_gradient, query_block)
        key_acc = lax.dynamic_update_slice_in_dim(key_acc, lax.dynamic_slice_in_dim(key_acc, start, window, 0) + key_portion, start, 0)
        value_acc = lax.dynamic_update_slice_in_dim(value_acc, lax.dynamic_slice_in_dim(value_acc, start, window, 0) + value_portion, start, 0)
        return ((key_acc, value_acc), query_portion.astype(jnp.bfloat16).reshape(block_len, head_count, head_width))
    empty = jnp.zeros((lead_rows + token_count, group_count, head_width), jnp.float32)
    (key_acc, value_acc), query_blocks = lax.scan(visit_block, (empty, empty), jnp.arange(token_count // block_len, dtype=jnp.int32))
    query_grad = query_blocks.reshape(token_count, head_count, head_width)
    key_grad = key_acc[lead_rows:].astype(jnp.bfloat16)
    value_grad = value_acc[lead_rows:].astype(jnp.bfloat16)
    return (query_grad, key_grad, value_grad)
```

```python
import functools
import math

import jax
import jax.numpy as jnp
from jax import lax
from jax.experimental import pallas as pl
from jax.experimental.pallas import tpu as pltpu
from jax.sharding import PartitionSpec as P

SPAN = 4
FILL = -1e30
TILE = 512
MESH = pl.DeviceIdType.MESH
F32 = jnp.float32
BF16 = jnp.bfloat16


def dot(a, b, dims):
    return lax.dot_general(a, b, (dims, ((), ())), preferred_element_type=F32)


def kernel(
    ctx_size, kv_size, block, per_group, scale,
    q_ref, k_ref, v_ref, do_ref, doc_ref,
    dq_ref, dk_ref, dv_ref,
    kbuf, vbuf, docbuf, lower, probs, dprobs, top, total, rowdot, weight, shift,
    ktrans, dq_acc, dk_acc, dv_acc, dk_out, dv_out, dk_in, dv_in,
    send_k, recv_k, send_v, recv_v, send_d, recv_d, send_gk, recv_gk, send_gv, recv_gv,
):
    tiles = q_ref.shape[0] // TILE
    toks = TILE // per_group
    ctx = lax.axis_index("ctx")
    kv = lax.axis_index("kv")

    def ahead(steps):
        return {"ctx": lax.rem(ctx + steps + ctx_size, ctx_size)}

    def beside(steps):
        return {"kv": lax.rem(kv + steps, kv_size)}

    barrier = pltpu.get_barrier_semaphore()
    for steps in range(1, SPAN):
        for sign in (1, -1):
            pl.semaphore_signal(barrier, inc=1, device_id=ahead(sign * steps), device_id_type=MESH)
    for steps in range(1, kv_size):
        pl.semaphore_signal(barrier, inc=1, device_id=beside(steps), device_id_type=MESH)
    docbuf[kv] = doc_ref[...]
    pl.semaphore_wait(barrier, 2 * (SPAN - 1) + kv_size - 1)

    doc_copies = []
    for steps in range(1, kv_size):
        doc_copies.append(
            pltpu.make_async_remote_copy(
                src_ref=doc_ref, dst_ref=docbuf.at[kv],
                send_sem=send_d.at[steps - 1], recv_sem=recv_d.at[steps - 1],
                device_id=beside(steps), device_id_type=MESH,
            )
        )
        doc_copies[-1].start()
    kv_copies = []
    for steps in range(1, SPAN):
        pair = []
        for src, dst, send, recv in ((k_ref, kbuf, send_k, recv_k), (v_ref, vbuf, send_v, recv_v)):
            pair.append(
                pltpu.make_async_remote_copy(
                    src_ref=src, dst_ref=dst.at[steps - 1],
                    send_sem=send.at[steps - 1], recv_sem=recv.at[steps - 1],
                    device_id=ahead(steps), device_id_type=MESH,
                )
            )
            pair[-1].start()
        kv_copies.append(pair)

    ktrans[0] = k_ref[...].T
    for copy in doc_copies:
        copy.wait()
    per_dev = docbuf.shape[1]
    for tile in range(tiles):
        parts = []
        for piece in range(TILE // 128):
            row = tile * (TILE // 128) + piece
            parts.append(docbuf[row // per_dev, pl.ds(row % per_dev, 1), :])
        lower[tile] = jnp.concatenate(parts, axis=1) - ctx * block

    def rows_of(tile):
        return pl.ds(pl.multiple_of(tile * TILE, TILE), TILE)

    def forward(offset, keys, values, key_count, tile):
        rows = rows_of(tile)
        position = lax.broadcasted_iota(jnp.int32, (key_count, TILE), 0)
        allowed = position >= lower[tile] + offset * block
        if offset == 0:
            token = tile * toks + lax.broadcasted_iota(jnp.int32, (1, TILE), 1) // per_group
            allowed = allowed & (position <= token)
        raw = dot(keys[pl.ds(0, key_count), :], q_ref[rows, :], ((1,), (1,)))
        scores = jnp.where(allowed, raw, FILL)
        highest = jnp.max(scores, axis=0, keepdims=True)
        unscaled = jnp.exp((scores - highest) * scale)
        gradient = dot(values[pl.ds(0, key_count), :], do_ref[rows, :], ((1,), (1,)))
        top[offset, tile] = highest
        total[offset, tile] = jnp.sum(unscaled, axis=0, keepdims=True)
        rowdot[offset, tile] = jnp.sum(unscaled * gradient, axis=0, keepdims=True)
        probs[offset, tile, pl.ds(0, key_count), :] = unscaled.astype(BF16)
        dprobs[offset, tile, pl.ds(0, key_count), :] = gradient.astype(BF16)

    def backward(offset, keys, key_count, tile):
        rows = rows_of(tile)
        w = weight[offset, tile].astype(BF16)
        r = shift[tile].astype(BF16)
        prob = probs[offset, tile, pl.ds(0, key_count), :] * w
        score = prob * (dprobs[offset, tile, pl.ds(0, key_count), :] - r)
        dv_acc[pl.ds(0, key_count), :] += dot(prob, do_ref[rows, :], ((1,), (0,)))
        dk_acc[pl.ds(0, key_count), :] += dot(score, q_ref[rows, :], ((1,), (0,)))
        part = dot(ktrans[offset, :, pl.ds(0, key_count)], score, ((1,), (0,)))
        if offset == SPAN - 1:
            dq_acc[tile] = part
        elif offset > 0:
            dq_acc[tile] += part
        else:
            dq_ref[rows, :] = ((dq_acc[tile] + part) * scale).T.astype(BF16)

    def over(first, last, body):
        def step(tile, carry):
            body(tile)
            return carry

        lax.fori_loop(first, last, step, 0)

    def over_own(body):
        half = tiles // 2
        over(0, half, functools.partial(body, block // 2))
        over(half, tiles, functools.partial(body, block))

    over_own(functools.partial(forward, 0, k_ref, v_ref))
    for offset in range(1, SPAN):
        for copy in kv_copies[offset - 1]:
            copy.wait()
        ktrans[offset] = kbuf[offset - 1].T
        over(0, tiles, functools.partial(forward, offset, kbuf.at[offset - 1], vbuf.at[offset - 1], block))

    def combine(tile):
        highest = top[0, tile]
        for offset in range(1, SPAN):
            highest = jnp.maximum(highest, top[offset, tile])
        factors = [jnp.exp((top[offset, tile] - highest) * scale) for offset in range(SPAN)]
        summed = factors[0] * total[0, tile]
        dotted = factors[0] * rowdot[0, tile]
        for offset in range(1, SPAN):
            summed += factors[offset] * total[offset, tile]
            dotted += factors[offset] * rowdot[offset, tile]
        inverse = 1.0 / summed
        shift[tile] = dotted * inverse
        for offset in range(SPAN):
            weight[offset, tile] = factors[offset] * inverse

    over(0, tiles, combine)

    grad_copies = []
    for offset in range(SPAN - 1, 0, -1):
        dk_acc[...] = jnp.zeros_like(dk_acc)
        dv_acc[...] = jnp.zeros_like(dv_acc)
        over(0, tiles, functools.partial(backward, offset, kbuf.at[offset - 1], block))
        slot = offset - 1
        dv_out[slot] = dv_acc[...].astype(BF16)
        dk_out[slot] = (dk_acc[...] * scale).astype(BF16)
        for src, dst, send, recv in (
            (dv_out, dv_in, send_gv, recv_gv),
            (dk_out, dk_in, send_gk, recv_gk),
        ):
            copy = pltpu.make_async_remote_copy(
                src_ref=src.at[slot], dst_ref=dst.at[slot],
                send_sem=send.at[slot], recv_sem=recv.at[slot],
                device_id=ahead(-offset), device_id_type=MESH,
            )
            copy.start()
            grad_copies.append(copy)
    dk_acc[...] = jnp.zeros_like(dk_acc)
    dv_acc[...] = jnp.zeros_like(dv_acc)
    over_own(functools.partial(backward, 0, k_ref))
    for copy in grad_copies:
        copy.wait()
    value = dv_acc[...]
    key = dk_acc[...] * scale
    for slot in range(SPAN - 1):
        value += dv_in[slot].astype(F32)
        key += dk_in[slot].astype(F32)
    dv_ref[...] = value.astype(BF16)
    dk_ref[...] = key.astype(BF16)


def local(ctx_size, kv_size, queries, key_heads, value_head_rows, out_grad, doc_start):
    block, heads, width = queries.shape
    rows = block * heads
    tiles = rows // TILE
    scale = 1.0 / math.sqrt(width)
    doc = jnp.repeat(doc_start, heads).reshape(-1, 128)
    vmem = pl.BlockSpec(memory_space=pltpu.VMEM)
    stat = (SPAN, tiles, 1, TILE)
    query_grad, key_grad, value_grad = pl.pallas_call(
        functools.partial(kernel, ctx_size, kv_size, block, heads, scale),
        out_shape=[
            jax.ShapeDtypeStruct((rows, width), BF16),
            jax.ShapeDtypeStruct((block, width), BF16),
            jax.ShapeDtypeStruct((block, width), BF16),
        ],
        in_specs=[vmem] * 5,
        out_specs=[vmem] * 3,
        scratch_shapes=[
            pltpu.VMEM((SPAN - 1, block, width), BF16),
            pltpu.VMEM((SPAN - 1, block, width), BF16),
            pltpu.VMEM((kv_size,) + doc.shape, jnp.int32),
            pltpu.VMEM((tiles, 1, TILE), jnp.int32),
            pltpu.VMEM((SPAN, tiles, block, TILE), BF16),
            pltpu.VMEM((SPAN, tiles, block, TILE), BF16),
            pltpu.VMEM(stat, F32),
            pltpu.VMEM(stat, F32),
            pltpu.VMEM(stat, F32),
            pltpu.VMEM(stat, F32),
            pltpu.VMEM(stat[1:], F32),
            pltpu.VMEM((SPAN, width, block), BF16),
            pltpu.VMEM((tiles, width, TILE), F32),
            pltpu.VMEM((block, width), F32),
            pltpu.VMEM((block, width), F32),
            pltpu.VMEM((SPAN - 1, block, width), BF16),
            pltpu.VMEM((SPAN - 1, block, width), BF16),
            pltpu.VMEM((SPAN - 1, block, width), BF16),
            pltpu.VMEM((SPAN - 1, block, width), BF16),
        ]
        + [pltpu.SemaphoreType.DMA((SPAN - 1,))] * 4
        + [pltpu.SemaphoreType.DMA((kv_size - 1,))] * 2
        + [pltpu.SemaphoreType.DMA((SPAN - 1,))] * 4,
        compiler_params=pltpu.CompilerParams(
            collective_id=0, has_side_effects=True, vmem_limit_bytes=56 * 1024 * 1024
        ),
        cost_estimate=pl.CostEstimate(
            flops=10 * rows * SPAN * block * width,
            bytes_accessed=8 * rows * width,
            transcendentals=rows * SPAN * block,
        ),
        name="attention_backward",
    )(
        queries.reshape(rows, width),
        key_heads.reshape(block, width),
        value_head_rows.reshape(block, width),
        out_grad.reshape(rows, width),
        doc,
    )
    return (
        query_grad.reshape(queries.shape),
        key_grad.reshape(key_heads.shape),
        value_grad.reshape(value_head_rows.shape),
    )


def solution(mesh):
    return jax.shard_map(
        functools.partial(local, mesh.shape["ctx"], mesh.shape["kv"]),
        mesh=mesh,
        in_specs=(
            P("ctx", "kv", None),
            P("ctx", "kv", None),
            P("ctx", "kv", None),
            P("ctx", "kv", None),
            P(("ctx", "kv")),
        ),
        out_specs=(P("ctx", "kv", None), P("ctx", "kv", None), P("ctx", "kv", None)),
        check_vma=False,
    )
```

```python
import functools
import math

import jax
import jax.numpy as jnp
from jax import lax
from jax.experimental import pallas as pl
from jax.experimental.pallas import tpu as pltpu
from jax.sharding import PartitionSpec as P

SPAN = 4
FILL = -1e30
TILE = 512
MESH = pl.DeviceIdType.MESH
F32 = jnp.float32
BF16 = jnp.bfloat16


def dot(a, b, dims):
    return lax.dot_general(a, b, (dims, ((), ())), preferred_element_type=F32)


def kernel(
    ctx_size, kv_size, block, per_group, scale,
    q_ref, k_ref, v_ref, do_ref, doc_ref,
    dq_ref, dk_ref, dv_ref,
    kbuf, vbuf, docbuf, lower, probs, dprobs, top, total, rowdot, weight, shift,
    ktrans, dq_acc, dk_acc, dv_acc, dk_out, dv_out, dk_in, dv_in,
    send_k, recv_k, send_v, recv_v, send_d, recv_d, send_gk, recv_gk, send_gv, recv_gv,
):
    tiles = q_ref.shape[0] // TILE
    toks = TILE // per_group
    base2 = scale * math.log2(math.e)
    ctx = lax.axis_index("ctx")
    kv = lax.axis_index("kv")

    def ahead(steps):
        return {"ctx": lax.rem(ctx + steps + ctx_size, ctx_size)}

    def beside(steps):
        return {"kv": lax.rem(kv + steps, kv_size)}

    barrier = pltpu.get_barrier_semaphore()
    for steps in range(1, SPAN):
        for sign in (1, -1):
            pl.semaphore_signal(barrier, inc=1, device_id=ahead(sign * steps), device_id_type=MESH)
    for steps in range(1, kv_size):
        pl.semaphore_signal(barrier, inc=1, device_id=beside(steps), device_id_type=MESH)
    docbuf[kv] = doc_ref[...]
    pl.semaphore_wait(barrier, 2 * (SPAN - 1) + kv_size - 1)

    doc_copies = []
    for steps in range(1, kv_size):
        doc_copies.append(
            pltpu.make_async_remote_copy(
                src_ref=doc_ref, dst_ref=docbuf.at[kv],
                send_sem=send_d.at[steps - 1], recv_sem=recv_d.at[steps - 1],
                device_id=beside(steps), device_id_type=MESH,
            )
        )
        doc_copies[-1].start()
    kv_copies = []
    for steps in range(1, SPAN):
        pair = []
        for src, dst, send, recv in ((k_ref, kbuf, send_k, recv_k), (v_ref, vbuf, send_v, recv_v)):
            pair.append(
                pltpu.make_async_remote_copy(
                    src_ref=src, dst_ref=dst.at[steps - 1],
                    send_sem=send.at[steps - 1], recv_sem=recv.at[steps - 1],
                    device_id=ahead(steps), device_id_type=MESH,
                )
            )
            pair[-1].start()
        kv_copies.append(pair)

    ktrans[0] = k_ref[...].T
    for copy in doc_copies:
        copy.wait()
    per_dev = docbuf.shape[1]
    for tile in range(tiles):
        parts = []
        for piece in range(TILE // 128):
            row = tile * (TILE // 128) + piece
            parts.append(docbuf[row // per_dev, pl.ds(row % per_dev, 1), :])
        lower[tile] = jnp.concatenate(parts, axis=1) - ctx * block

    def rows_of(tile):
        return pl.ds(pl.multiple_of(tile * TILE, TILE), TILE)

    def forward(offset, keys, values, key_count, tile):
        rows = rows_of(tile)
        position = lax.broadcasted_iota(jnp.int32, (key_count, TILE), 0)
        allowed = position >= lower[tile] + offset * block
        if offset == 0:
            token = tile * toks + lax.broadcasted_iota(jnp.int32, (1, TILE), 1) // per_group
            allowed = allowed & (position <= token)
        raw = dot(keys[pl.ds(0, key_count), :], q_ref[rows, :], ((1,), (1,)))
        scores = jnp.where(allowed, raw, FILL)
        highest = jnp.max(scores, axis=0, keepdims=True)
        unscaled = jnp.exp2((scores - highest) * base2)
        gradient = dot(values[pl.ds(0, key_count), :], do_ref[rows, :], ((1,), (1,)))
        top[offset, tile] = highest
        total[offset, tile] = jnp.sum(unscaled, axis=0, keepdims=True)
        rowdot[offset, tile] = jnp.sum(unscaled * gradient, axis=0, keepdims=True)
        probs[offset, tile, pl.ds(0, key_count), :] = unscaled.astype(BF16)
        dprobs[offset, tile, pl.ds(0, key_count), :] = gradient.astype(BF16)

    def backward(offset, keys, key_count, tile):
        rows = rows_of(tile)
        w = weight[offset, tile].astype(BF16)
        r = shift[tile].astype(BF16)
        prob = probs[offset, tile, pl.ds(0, key_count), :] * w
        score = prob * (dprobs[offset, tile, pl.ds(0, key_count), :] - r)
        dv_acc[pl.ds(0, key_count), :] += dot(prob, do_ref[rows, :], ((1,), (0,)))
        dk_acc[pl.ds(0, key_count), :] += dot(score, q_ref[rows, :], ((1,), (0,)))
        part = dot(ktrans[offset, :, pl.ds(0, key_count)], score, ((1,), (0,)))
        if offset == SPAN - 1:
            dq_acc[tile] = part
        elif offset > 0:
            dq_acc[tile] += part
        else:
            dq_ref[rows, :] = ((dq_acc[tile] + part) * scale).T.astype(BF16)

    def over(first, last, body):
        def step(pair, carry):
            body(first + 2 * pair)
            body(first + 2 * pair + 1)
            return carry

        lax.fori_loop(0, (last - first) // 2, step, 0)

    def over_own(body):
        half = tiles // 2
        over(0, half, functools.partial(body, block // 2))
        over(half, tiles, functools.partial(body, block))

    over_own(functools.partial(forward, 0, k_ref, v_ref))
    for offset in range(1, SPAN):
        for copy in kv_copies[offset - 1]:
            copy.wait()
        ktrans[offset] = kbuf[offset - 1].T
        over(0, tiles, functools.partial(forward, offset, kbuf.at[offset - 1], vbuf.at[offset - 1], block))

    def combine(tile):
        highest = top[0, tile]
        for offset in range(1, SPAN):
            highest = jnp.maximum(highest, top[offset, tile])
        factors = [jnp.exp2((top[offset, tile] - highest) * base2) for offset in range(SPAN)]
        summed = factors[0] * total[0, tile]
        dotted = factors[0] * rowdot[0, tile]
        for offset in range(1, SPAN):
            summed += factors[offset] * total[offset, tile]
            dotted += factors[offset] * rowdot[offset, tile]
        inverse = 1.0 / summed
        shift[tile] = dotted * inverse
        for offset in range(SPAN):
            weight[offset, tile] = factors[offset] * inverse

    over(0, tiles, combine)

    grad_copies = []
    for offset in range(SPAN - 1, 0, -1):
        dk_acc[...] = jnp.zeros_like(dk_acc)
        dv_acc[...] = jnp.zeros_like(dv_acc)
        over(0, tiles, functools.partial(backward, offset, kbuf.at[offset - 1], block))
        slot = offset - 1
        dv_out[slot] = dv_acc[...].astype(BF16)
        dk_out[slot] = (dk_acc[...] * scale).astype(BF16)
        for src, dst, send, recv in (
            (dv_out, dv_in, send_gv, recv_gv),
            (dk_out, dk_in, send_gk, recv_gk),
        ):
            copy = pltpu.make_async_remote_copy(
                src_ref=src.at[slot], dst_ref=dst.at[slot],
                send_sem=send.at[slot], recv_sem=recv.at[slot],
                device_id=ahead(-offset), device_id_type=MESH,
            )
            copy.start()
            grad_copies.append(copy)
    dk_acc[...] = jnp.zeros_like(dk_acc)
    dv_acc[...] = jnp.zeros_like(dv_acc)
    over_own(functools.partial(backward, 0, k_ref))
    for copy in grad_copies:
        copy.wait()
    value = dv_acc[...]
    key = dk_acc[...] * scale
    for slot in range(SPAN - 1):
        value += dv_in[slot].astype(F32)
        key += dk_in[slot].astype(F32)
    dv_ref[...] = value.astype(BF16)
    dk_ref[...] = key.astype(BF16)


def hand_over(dq_in, dk_in, dv_in, dq_out, dk_out, dv_out, sems):
    rows = dq_in.shape[0] // 4
    pairs = [(dq_in.at[pl.ds(i * rows, rows), :], dq_out.at[pl.ds(i * rows, rows), :]) for i in range(4)]
    pairs += [(dk_in, dk_out), (dv_in, dv_out)]
    copies = [pltpu.make_async_copy(src, dst, sems.at[i]) for i, (src, dst) in enumerate(pairs)]
    for copy in copies:
        copy.start()
    for copy in copies:
        copy.wait()


def local(ctx_size, kv_size, queries, key_heads, value_head_rows, out_grad, doc_start):
    block, heads, width = queries.shape
    rows = block * heads
    tiles = rows // TILE
    scale = 1.0 / math.sqrt(width)
    doc = jnp.repeat(doc_start, heads).reshape(-1, 128)
    vmem = pl.BlockSpec(memory_space=pltpu.VMEM)
    stat = (SPAN, tiles, 1, TILE)
    results = pl.pallas_call(
        functools.partial(kernel, ctx_size, kv_size, block, heads, scale),
        out_shape=[
            jax.ShapeDtypeStruct((rows, width), BF16),
            jax.ShapeDtypeStruct((block, width), BF16),
            jax.ShapeDtypeStruct((block, width), BF16),
        ],
        in_specs=[vmem] * 5,
        out_specs=[vmem] * 3,
        scratch_shapes=[
            pltpu.VMEM((SPAN - 1, block, width), BF16),
            pltpu.VMEM((SPAN - 1, block, width), BF16),
            pltpu.VMEM((kv_size,) + doc.shape, jnp.int32),
            pltpu.VMEM((tiles, 1, TILE), jnp.int32),
            pltpu.VMEM((SPAN, tiles, block, TILE), BF16),
            pltpu.VMEM((SPAN, tiles, block, TILE), BF16),
            pltpu.VMEM(stat, F32),
            pltpu.VMEM(stat, F32),
            pltpu.VMEM(stat, F32),
            pltpu.VMEM(stat, F32),
            pltpu.VMEM(stat[1:], F32),
            pltpu.VMEM((SPAN, width, block), BF16),
            pltpu.VMEM((tiles, width, TILE), F32),
            pltpu.VMEM((block, width), F32),
            pltpu.VMEM((block, width), F32),
            pltpu.VMEM((SPAN - 1, block, width), BF16),
            pltpu.VMEM((SPAN - 1, block, width), BF16),
            pltpu.VMEM((SPAN - 1, block, width), BF16),
            pltpu.VMEM((SPAN - 1, block, width), BF16),
        ]
        + [pltpu.SemaphoreType.DMA((SPAN - 1,))] * 4
        + [pltpu.SemaphoreType.DMA((kv_size - 1,))] * 2
        + [pltpu.SemaphoreType.DMA((SPAN - 1,))] * 4,
        compiler_params=pltpu.CompilerParams(
            collective_id=0, has_side_effects=True, vmem_limit_bytes=56 * 1024 * 1024
        ),
        cost_estimate=pl.CostEstimate(
            flops=10 * rows * SPAN * block * width,
            bytes_accessed=8 * rows * width,
            transcendentals=rows * SPAN * block,
        ),
        name="attention_backward",
    )(
        queries.reshape(rows, width),
        key_heads.reshape(block, width),
        value_head_rows.reshape(block, width),
        out_grad.reshape(rows, width),
        doc,
    )
    query_grad, key_grad, value_grad = pl.pallas_call(
        hand_over,
        out_shape=[jax.ShapeDtypeStruct(x.shape, x.dtype) for x in results],
        in_specs=[pl.BlockSpec(memory_space=pl.ANY)] * 3,
        out_specs=[pl.BlockSpec(memory_space=pl.ANY)] * 3,
        scratch_shapes=[pltpu.SemaphoreType.DMA((6,))],
        name="hand_over",
    )(*results)
    return (
        query_grad.reshape(queries.shape),
        key_grad.reshape(key_heads.shape),
        value_grad.reshape(value_head_rows.shape),
    )


def solution(mesh):
    return jax.shard_map(
        functools.partial(local, mesh.shape["ctx"], mesh.shape["kv"]),
        mesh=mesh,
        in_specs=(
            P("ctx", "kv", None),
            P("ctx", "kv", None),
            P("ctx", "kv", None),
            P("ctx", "kv", None),
            P(("ctx", "kv")),
        ),
        out_specs=(P("ctx", "kv", None), P("ctx", "kv", None), P("ctx", "kv", None)),
        check_vma=False,
    )
```

```python
import functools
import math

import jax
import jax.numpy as jnp
from jax import lax
from jax.experimental import pallas as pl
from jax.experimental.pallas import tpu as pltpu
from jax.sharding import PartitionSpec as P

SPAN = 4
FILL = -1e30
TILE = 512
SUB = 128
LANES = 128
STEPS = 4
MESH = pl.DeviceIdType.MESH
F32 = jnp.float32
BF16 = jnp.bfloat16


def dot(a, b, dims):
    return lax.dot_general(a, b, (dims, ((), ())), preferred_element_type=F32)


def kernel(
    ctx_size, kv_size, block, per_group, scale,
    q_ref, k_ref, v_ref, do_ref, doc_ref,
    dq_ref, dk_ref, dv_ref,
    kbuf, vbuf, docbuf, lower, probs, dprobs, top, total, rowdot, weight, shift,
    ktrans, dq_acc, dk_acc, dv_acc, dk_out, dv_out, dk_in, dv_in,
    send_k, recv_k, send_v, recv_v, send_d, recv_d, send_gk, recv_gk, send_gv, recv_gv,
):
    tiles = q_ref.shape[0] // TILE
    toks = TILE // per_group
    subs = block // SUB
    base2 = scale * math.log2(math.e)
    ctx = lax.axis_index("ctx")
    kv = lax.axis_index("kv")
    odd = lax.rem(ctx, 2)

    def ahead(steps):
        return {"ctx": lax.rem(ctx + steps + ctx_size, ctx_size)}

    def beside(steps):
        return {"kv": lax.rem(kv + steps, kv_size)}

    partner = {"ctx": ctx + 1 - 2 * odd}

    barrier = pltpu.get_barrier_semaphore()
    for steps in (1, -1, 3, -3):
        pl.semaphore_signal(barrier, inc=1, device_id=ahead(steps), device_id_type=MESH)
    for steps in range(1, kv_size):
        pl.semaphore_signal(barrier, inc=1, device_id=beside(steps), device_id_type=MESH)
    docbuf[kv] = doc_ref[...]
    pl.semaphore_wait(barrier, 4 + kv_size - 1)

    doc_copies = []
    for steps in range(1, kv_size):
        doc_copies.append(
            pltpu.make_async_remote_copy(
                src_ref=doc_ref, dst_ref=docbuf.at[kv],
                send_sem=send_d.at[steps - 1], recv_sem=recv_d.at[steps - 1],
                device_id=beside(steps), device_id_type=MESH,
            )
        )
        doc_copies[-1].start()

    def both(sources, targets, slot, sends, recvs, device):
        return [
            pltpu.make_async_remote_copy(
                src_ref=src, dst_ref=dst.at[slot],
                send_sem=send.at[slot], recv_sem=recv.at[slot],
                device_id=device, device_id_type=MESH,
            )
            for src, dst, send, recv in zip(sources, targets, sends, recvs)
        ]

    def start(copies):
        for copy in copies:
            copy.start()

    def received(copies):
        for copy in copies:
            copy.wait_recv()

    kv_buffers = ((kbuf, vbuf), (send_k, send_v), (recv_k, recv_v))
    one, three = [
        both((k_ref, v_ref), kv_buffers[0], steps - 1, kv_buffers[1], kv_buffers[2], ahead(steps))
        for steps in (1, 3)
    ]
    start(one)
    start(three)
    passed_on = both(
        (kbuf.at[2 * odd], vbuf.at[2 * odd]), kv_buffers[0], 1, kv_buffers[1], kv_buffers[2], partner
    )

    ktrans[0] = k_ref[...].T
    top[...] = jnp.full_like(top, FILL)
    total[...] = jnp.zeros_like(total)
    rowdot[...] = jnp.zeros_like(rowdot)
    for copy in doc_copies:
        copy.wait()
    per_dev = docbuf.shape[1]
    for tile in range(tiles):
        parts = []
        for piece in range(TILE // 128):
            row = tile * (TILE // 128) + piece
            parts.append(docbuf[row // per_dev, pl.ds(row % per_dev, 1), :])
        lower[tile] = jnp.concatenate(parts, axis=1) - ctx * block

    def rows_of(tile):
        return pl.ds(pl.multiple_of(tile * TILE, TILE), TILE)

    def forward(offset, keys, values, key_count, tile):
        rows = rows_of(tile)
        raw = dot(keys[pl.ds(0, key_count), :], q_ref[rows, :], ((1,), (1,)))
        gradient = dot(values[pl.ds(0, key_count), :], do_ref[rows, :], ((1,), (1,)))
        first = lower[tile] + offset * block
        position = lax.broadcasted_iota(jnp.int32, (SUB, LANES), 0)
        lane_token = lax.broadcasted_iota(jnp.int32, (1, LANES), 1) // per_group
        for lane in range(0, TILE, LANES):
            lanes = slice(lane, lane + LANES)
            for sub in range(key_count // SUB):
                part = slice(sub * SUB, (sub + 1) * SUB)
                allowed = position >= first[:, lanes] - sub * SUB
                if offset == 0:
                    token = lane_token + (tile * toks + lane // per_group - sub * SUB)
                    allowed = allowed & (position <= token)
                scores = jnp.where(allowed, raw[part, lanes], FILL)
                highest = jnp.max(scores, axis=0, keepdims=True)
                unscaled = jnp.exp2((scores - highest) * base2)
                line = pl.ds(offset * subs + sub, 1)
                chunk = gradient[part, lanes]
                top[tile, line, lanes] = highest
                total[tile, line, lanes] = jnp.sum(unscaled, axis=0, keepdims=True)
                rowdot[tile, line, lanes] = jnp.sum(unscaled * chunk, axis=0, keepdims=True)
                probs[offset, tile, pl.ds(sub * SUB, SUB), lanes] = unscaled.astype(BF16)
                dprobs[offset, tile, pl.ds(sub * SUB, SUB), lanes] = chunk.astype(BF16)

    def backward(offset, first, keys, key_count, tile):
        rows = rows_of(tile)
        r = shift[tile].astype(BF16)
        prob_parts = []
        score_parts = []
        for sub in range(key_count // SUB):
            part = pl.ds(sub * SUB, SUB)
            w = weight[tile, pl.ds(offset * subs + sub, 1), :].astype(BF16)
            prob_parts.append(probs[offset, tile, part, :] * w)
            score_parts.append(prob_parts[-1] * (dprobs[offset, tile, part, :] - r))
        prob = jnp.concatenate(prob_parts, axis=0)
        score = jnp.concatenate(score_parts, axis=0)
        dv_acc[pl.ds(0, key_count), :] += dot(prob, do_ref[rows, :], ((1,), (0,)))
        dk_acc[pl.ds(0, key_count), :] += dot(score, q_ref[rows, :], ((1,), (0,)))
        part = dot(ktrans[offset, :, pl.ds(0, key_count)], score, ((1,), (0,)))
        if first:
            dq_acc[tile] = part
        elif offset > 0:
            dq_acc[tile] += part
        else:
            dq_ref[rows, :] = ((dq_acc[tile] + part) * scale).T.astype(BF16)

    def over(body):
        def step(pair, carry):
            body(2 * pair)
            body(2 * pair + 1)
            return carry

        lax.fori_loop(0, tiles // 2, step, 0)

    def over_own(body):
        for tile in range(tiles):
            body(SUB * (((tile + 1) * toks + SUB - 1) // SUB), tile)

    def visit(offset):
        ktrans[offset] = kbuf[offset - 1].T
        over(functools.partial(forward, offset, kbuf.at[offset - 1], vbuf.at[offset - 1], block))

    over_own(functools.partial(forward, 0, k_ref, v_ref))
    received(one)

    @pl.when(odd == 0)
    def _():
        start(passed_on)

    visit(1)
    received(three)

    @pl.when(odd == 1)
    def _():
        start(passed_on)

    visit(3)
    received(passed_on)
    visit(2)

    def combine(tile):
        tops = top[tile]
        factors = jnp.exp2((tops - jnp.max(tops, axis=0, keepdims=True)) * base2)
        inverse = 1.0 / jnp.sum(factors * total[tile], axis=0, keepdims=True)
        shift[tile] = jnp.sum(factors * rowdot[tile], axis=0, keepdims=True) * inverse
        weight[tile] = factors * inverse

    over(combine)

    def accumulate(offset, first):
        dk_acc[...] = jnp.zeros_like(dk_acc)
        dv_acc[...] = jnp.zeros_like(dv_acc)
        over(functools.partial(backward, offset, first, kbuf.at[offset - 1], block))
        dk_acc[...] = dk_acc[...] * scale

    grad_sends, grad_recvs = (send_gk, send_gv), (recv_gk, recv_gv)

    def give(offset, device):
        slot = offset - 1
        dk_out[slot] = dk_acc[...].astype(BF16)
        dv_out[slot] = dv_acc[...].astype(BF16)
        copies = both(
            (dk_out.at[slot], dv_out.at[slot]), (dk_in, dv_in), slot, grad_sends, grad_recvs, device
        )
        start(copies)
        return copies

    def take(slot):
        dk_acc[...] += dk_in[slot].astype(F32)
        dv_acc[...] += dv_in[slot].astype(F32)

    accumulate(2, True)
    given_two = give(2, partner)
    accumulate(3, False)

    @pl.when(odd == 1)
    def _():
        received(given_two)
        take(1)

    given_three = give(3, ahead(-3))
    accumulate(1, False)

    @pl.when(odd == 0)
    def _():
        received(given_two)
        take(1)

    given_one = give(1, ahead(-1))
    dk_acc[...] = jnp.zeros_like(dk_acc)
    dv_acc[...] = jnp.zeros_like(dv_acc)
    over_own(functools.partial(backward, 0, False, k_ref))
    dk_acc[...] = dk_acc[...] * scale
    received(given_three)
    take(2)
    received(given_one)
    take(0)
    dv_ref[...] = dv_acc[...].astype(BF16)
    dk_ref[...] = dk_acc[...].astype(BF16)
    for copies in (one, three, passed_on, given_two, given_three, given_one):
        for copy in copies:
            copy.wait_send()


def hand_over(dq_in, dk_in, dv_in, dq_out, dk_out, dv_out):
    dq_out[...] = dq_in[...]
    dk_out[...] = dk_in[...]
    dv_out[...] = dv_in[...]


def local(ctx_size, kv_size, queries, key_heads, value_head_rows, out_grad, doc_start):
    block, heads, width = queries.shape
    rows = block * heads
    tiles = rows // TILE
    scale = 1.0 / math.sqrt(width)
    doc = jnp.repeat(doc_start, heads).reshape(-1, 128)
    vmem = pl.BlockSpec(memory_space=pltpu.VMEM)
    stat = (tiles, SPAN * (block // SUB), TILE)
    results = pl.pallas_call(
        functools.partial(kernel, ctx_size, kv_size, block, heads, scale),
        out_shape=[
            jax.ShapeDtypeStruct((rows, width), BF16),
            jax.ShapeDtypeStruct((block, width), BF16),
            jax.ShapeDtypeStruct((block, width), BF16),
        ],
        in_specs=[vmem] * 5,
        out_specs=[vmem] * 3,
        scratch_shapes=[
            pltpu.VMEM((SPAN - 1, block, width), BF16),
            pltpu.VMEM((SPAN - 1, block, width), BF16),
            pltpu.VMEM((kv_size,) + doc.shape, jnp.int32),
            pltpu.VMEM((tiles, 1, TILE), jnp.int32),
            pltpu.VMEM((SPAN, tiles, block, TILE), BF16),
            pltpu.VMEM((SPAN, tiles, block, TILE), BF16),
            pltpu.VMEM(stat, F32),
            pltpu.VMEM(stat, F32),
            pltpu.VMEM(stat, F32),
            pltpu.VMEM(stat, F32),
            pltpu.VMEM((tiles, 1, TILE), F32),
            pltpu.VMEM((SPAN, width, block), BF16),
            pltpu.VMEM((tiles, width, TILE), F32),
            pltpu.VMEM((block, width), F32),
            pltpu.VMEM((block, width), F32),
            pltpu.VMEM((SPAN - 1, block, width), BF16),
            pltpu.VMEM((SPAN - 1, block, width), BF16),
            pltpu.VMEM((SPAN - 1, block, width), BF16),
            pltpu.VMEM((SPAN - 1, block, width), BF16),
        ]
        + [pltpu.SemaphoreType.DMA((SPAN - 1,))] * 4
        + [pltpu.SemaphoreType.DMA((kv_size - 1,))] * 2
        + [pltpu.SemaphoreType.DMA((SPAN - 1,))] * 4,
        compiler_params=pltpu.CompilerParams(
            collective_id=0, has_side_effects=True, vmem_limit_bytes=56 * 1024 * 1024
        ),
        cost_estimate=pl.CostEstimate(
            flops=10 * rows * SPAN * block * width,
            bytes_accessed=8 * rows * width,
            transcendentals=rows * SPAN * block,
        ),
        name="attention_backward",
    )(
        queries.reshape(rows, width),
        key_heads.reshape(block, width),
        value_head_rows.reshape(block, width),
        out_grad.reshape(rows, width),
        doc,
    )
    specs = [pl.BlockSpec((x.shape[0] // STEPS, width), lambda i: (i, 0)) for x in results]
    query_grad, key_grad, value_grad = pl.pallas_call(
        hand_over,
        out_shape=[jax.ShapeDtypeStruct(x.shape, x.dtype) for x in results],
        grid=(STEPS,),
        in_specs=specs,
        out_specs=specs,
        name="hand_over",
    )(*results)
    return (
        query_grad.reshape(queries.shape),
        key_grad.reshape(key_heads.shape),
        value_grad.reshape(value_head_rows.shape),
    )


def solution(mesh):
    return jax.shard_map(
        functools.partial(local, mesh.shape["ctx"], mesh.shape["kv"]),
        mesh=mesh,
        in_specs=(
            P("ctx", "kv", None),
            P("ctx", "kv", None),
            P("ctx", "kv", None),
            P("ctx", "kv", None),
            P(("ctx", "kv")),
        ),
        out_specs=(P("ctx", "kv", None), P("ctx", "kv", None), P("ctx", "kv", None)),
        check_vma=False,
    )
```

```python
import functools
import math

import jax
import jax.numpy as jnp
from jax import lax
from jax.experimental import pallas as pl
from jax.experimental.pallas import tpu as pltpu
from jax.sharding import PartitionSpec as P

SPAN = 4
FILL = -1e30
TILE = 512
SUB = 128
LANES = 128
HALF = 256
STEPS = 4
MESH = pl.DeviceIdType.MESH
F32 = jnp.float32
BF16 = jnp.bfloat16


def dot(a, b, dims):
    return lax.dot_general(a, b, (dims, ((), ())), preferred_element_type=F32)


def kernel(
    ctx_size, kv_size, block, per_group, scale,
    q_any, k_any, v_any, do_any, doc_any,
    dq_any, dk_ref, dv_ref,
    q_ref, k_ref, v_ref, do_ref, dq_ref, s_even, s_odd, p_even, p_odd,
    kbuf, vbuf, docbuf, lower, probs, dprobs, top, total, rowdot, weight, shift,
    ktrans, dq_acc, dk_acc, dv_acc, dk_out, dv_out, dk_in, dv_in,
    send_k, recv_k, send_v, recv_v, send_d, recv_d, send_gk, recv_gk, send_gv, recv_gv,
    load_sem, store_sem,
):
    tiles = q_ref.shape[0] // TILE
    toks = TILE // per_group
    subs = block // SUB
    base2 = scale * math.log2(math.e)
    ctx = lax.axis_index("ctx")
    kv = lax.axis_index("kv")
    odd = lax.rem(ctx, 2)

    def ahead(steps):
        return {"ctx": lax.rem(ctx + steps + ctx_size, ctx_size)}

    def beside(steps):
        return {"kv": lax.rem(kv + steps, kv_size)}

    loads = [
        pltpu.make_async_copy(src, dst, load_sem.at[i])
        for i, (src, dst) in enumerate(
            (
                (doc_any, docbuf.at[kv]), (k_any, k_ref), (q_any, q_ref),
                (v_any, v_ref), (do_any, do_ref),
            )
        )
    ]
    for copy in loads:
        copy.start()

    partner = {"ctx": ctx + 1 - 2 * odd}

    barrier = pltpu.get_barrier_semaphore()
    for steps in (1, -1, 3, -3):
        pl.semaphore_signal(barrier, inc=1, device_id=ahead(steps), device_id_type=MESH)
    for steps in range(1, kv_size):
        pl.semaphore_signal(barrier, inc=1, device_id=beside(steps), device_id_type=MESH)
    pl.semaphore_wait(barrier, 4 + kv_size - 1)

    doc_copies = []
    for steps in range(1, kv_size):
        doc_copies.append(
            pltpu.make_async_remote_copy(
                src_ref=doc_any, dst_ref=docbuf.at[kv],
                send_sem=send_d.at[steps - 1], recv_sem=recv_d.at[steps - 1],
                device_id=beside(steps), device_id_type=MESH,
            )
        )
        doc_copies[-1].start()

    def both(sources, targets, slot, sends, recvs, device):
        return [
            pltpu.make_async_remote_copy(
                src_ref=src, dst_ref=dst.at[slot],
                send_sem=send.at[slot], recv_sem=recv.at[slot],
                device_id=device, device_id_type=MESH,
            )
            for src, dst, send, recv in zip(sources, targets, sends, recvs)
        ]

    def start(copies):
        for copy in copies:
            copy.start()

    def received(copies):
        for copy in copies:
            copy.wait_recv()

    kv_buffers = ((kbuf, vbuf), (send_k, send_v), (recv_k, recv_v))
    one, three = [
        both((k_any, v_any), kv_buffers[0], steps - 1, kv_buffers[1], kv_buffers[2], ahead(steps))
        for steps in (1, 3)
    ]
    start(one)
    start(three)
    passed_on = both(
        (kbuf.at[2 * odd], vbuf.at[2 * odd]), kv_buffers[0], 1, kv_buffers[1], kv_buffers[2], partner
    )

    for copy in loads:
        copy.wait()
    ktrans[0] = k_ref[...].T
    top[...] = jnp.full_like(top, FILL)
    total[...] = jnp.zeros_like(total)
    rowdot[...] = jnp.zeros_like(rowdot)
    for copy in doc_copies:
        copy.wait()
    per_dev = docbuf.shape[1]
    for tile in range(tiles):
        parts = []
        for piece in range(TILE // 128):
            row = tile * (TILE // 128) + piece
            parts.append(docbuf[row // per_dev, pl.ds(row % per_dev, 1), :])
        lower[tile] = jnp.concatenate(parts, axis=1) - ctx * block

    def rows_of(tile):
        return pl.ds(pl.multiple_of(tile * TILE, TILE), TILE)

    def products(keys, values, key_count, tile, lane, held):
        s_ref, p_ref = held
        rows = pl.ds(pl.multiple_of(tile * TILE + lane, HALF), HALF)
        lanes = slice(lane, lane + HALF)
        count = pl.ds(0, key_count)
        s_ref[count, lanes] = dot(keys[count, :], q_ref[rows, :], ((1,), (1,)))
        p_ref[count, lanes] = dot(values[count, :], do_ref[rows, :], ((1,), (1,))).astype(BF16)

    def softmax(offset, key_count, tile, start_lane, held):
        s_ref, p_ref = held
        first = lower[tile] + offset * block
        position = lax.broadcasted_iota(jnp.int32, (SUB, LANES), 0)
        lane_token = lax.broadcasted_iota(jnp.int32, (1, LANES), 1) // per_group
        for lane in range(start_lane, start_lane + HALF, LANES):
            lanes = slice(lane, lane + LANES)
            for sub in range(key_count // SUB):
                part = pl.ds(sub * SUB, SUB)
                allowed = position >= first[:, lanes] - sub * SUB
                if offset == 0:
                    token = lane_token + (tile * toks + lane // per_group - sub * SUB)
                    allowed = allowed & (position <= token)
                scores = jnp.where(allowed, s_ref[part, lanes], FILL)
                highest = jnp.max(scores, axis=0, keepdims=True)
                unscaled = jnp.exp2((scores - highest) * base2)
                line = pl.ds(offset * subs + sub, 1)
                chunk = p_ref[part, lanes]
                top[tile, line, lanes] = highest
                total[tile, line, lanes] = jnp.sum(unscaled, axis=0, keepdims=True)
                rowdot[tile, line, lanes] = jnp.sum(
                    unscaled * chunk.astype(F32), axis=0, keepdims=True
                )
                probs[offset, tile, part, lanes] = unscaled.astype(BF16)
                dprobs[offset, tile, part, lanes] = chunk

    def forward(offset, keys, values, now, later):
        tile, count, held = now
        for lane in range(0, TILE, HALF):
            if later is not None:
                products(keys, values, later[1], later[0], lane, later[2])
            softmax(offset, count, tile, lane, held)

    even, unequal = (s_even, p_even), (s_odd, p_odd)

    def backward(offset, first, keys, key_count, tile):
        rows = rows_of(tile)
        r = shift[tile].astype(BF16)
        prob_parts = []
        score_parts = []
        for sub in range(key_count // SUB):
            part = pl.ds(sub * SUB, SUB)
            w = weight[tile, pl.ds(offset * subs + sub, 1), :].astype(BF16)
            prob_parts.append(probs[offset, tile, part, :] * w)
            score_parts.append(prob_parts[-1] * (dprobs[offset, tile, part, :] - r))
        prob = jnp.concatenate(prob_parts, axis=0)
        score = jnp.concatenate(score_parts, axis=0)
        dv_acc[pl.ds(0, key_count), :] += dot(prob, do_ref[rows, :], ((1,), (0,)))
        dk_acc[pl.ds(0, key_count), :] += dot(score, q_ref[rows, :], ((1,), (0,)))
        part = dot(ktrans[offset, :, pl.ds(0, key_count)], score, ((1,), (0,)))
        if first:
            dq_acc[tile] = part
        elif offset > 0:
            dq_acc[tile] += part
        else:
            dq_ref[rows, :] = ((dq_acc[tile] + part) * scale).T.astype(BF16)
            stores[tile].start()

    stores = [
        pltpu.make_async_copy(
            dq_ref.at[pl.ds(tile * TILE, TILE), :], dq_any.at[pl.ds(tile * TILE, TILE), :], store_sem.at[tile]
        )
        for tile in range(tiles)
    ]

    def over(body):
        def step(pair, carry):
            body(2 * pair)
            body(2 * pair + 1)
            return carry

        lax.fori_loop(0, tiles // 2, step, 0)

    def over_own(body):
        for tile in range(tiles):
            body(SUB * (((tile + 1) * toks + SUB - 1) // SUB), tile)

    def visit(offset):
        keys, values = kbuf.at[offset - 1], vbuf.at[offset - 1]
        ktrans[offset] = keys[...].T
        for lane in range(0, TILE, HALF):
            products(keys, values, block, 0, lane, even)

        def step(pair, carry):
            tile = 2 * pair
            after = jnp.minimum(tile + 2, tiles - 1)
            forward(offset, keys, values, (tile, block, even), (tile + 1, block, unequal))
            forward(offset, keys, values, (tile + 1, block, unequal), (after, block, even))
            return carry

        lax.fori_loop(0, tiles // 2, step, 0)

    own = []
    over_own(lambda count, tile: own.append((tile, count, (even, unequal)[tile % 2])))
    for lane in range(0, TILE, HALF):
        products(k_ref, v_ref, own[0][1], 0, lane, even)
    for now, later in zip(own, own[1:] + [None]):
        forward(0, k_ref, v_ref, now, later)
    received(one)

    @pl.when(odd == 0)
    def _():
        start(passed_on)

    visit(1)
    received(three)

    @pl.when(odd == 1)
    def _():
        start(passed_on)

    visit(3)
    received(passed_on)
    visit(2)

    def combine(tile):
        tops = top[tile]
        factors = jnp.exp2((tops - jnp.max(tops, axis=0, keepdims=True)) * base2)
        inverse = 1.0 / jnp.sum(factors * total[tile], axis=0, keepdims=True)
        shift[tile] = jnp.sum(factors * rowdot[tile], axis=0, keepdims=True) * inverse
        weight[tile] = factors * inverse

    over(combine)

    def accumulate(offset, first):
        dk_acc[...] = jnp.zeros_like(dk_acc)
        dv_acc[...] = jnp.zeros_like(dv_acc)
        over(functools.partial(backward, offset, first, kbuf.at[offset - 1], block))
        dk_acc[...] = dk_acc[...] * scale

    grad_sends, grad_recvs = (send_gk, send_gv), (recv_gk, recv_gv)

    def give(offset, device):
        slot = offset - 1
        dk_out[slot] = dk_acc[...].astype(BF16)
        dv_out[slot] = dv_acc[...].astype(BF16)
        copies = both(
            (dk_out.at[slot], dv_out.at[slot]), (dk_in, dv_in), slot, grad_sends, grad_recvs, device
        )
        start(copies)
        return copies

    def take(slot):
        dk_acc[...] += dk_in[slot].astype(F32)
        dv_acc[...] += dv_in[slot].astype(F32)

    accumulate(2, True)
    given_two = give(2, partner)
    accumulate(3, False)

    @pl.when(odd == 1)
    def _():
        received(given_two)
        take(1)

    given_three = give(3, ahead(-3))
    accumulate(1, False)

    @pl.when(odd == 0)
    def _():
        received(given_two)
        take(1)

    given_one = give(1, ahead(-1))
    dk_acc[...] = jnp.zeros_like(dk_acc)
    dv_acc[...] = jnp.zeros_like(dv_acc)
    over_own(functools.partial(backward, 0, False, k_ref))
    dk_acc[...] = dk_acc[...] * scale
    received(given_three)
    take(2)
    received(given_one)
    take(0)
    dv_ref[...] = dv_acc[...].astype(BF16)
    dk_ref[...] = dk_acc[...].astype(BF16)
    for copies in (one, three, passed_on, given_two, given_three, given_one):
        for copy in copies:
            copy.wait_send()
    for copy in stores:
        copy.wait()


def hand_over(dq_in, dk_in, dv_in, dq_out, dk_out, dv_out, dq_mid, dk_mid, dv_mid, sems):
    parts = [(dk_in, dk_mid, dk_out), (dv_in, dv_mid, dv_out)]
    rows = dq_in.shape[0] // STEPS
    for step in range(STEPS):
        part = pl.ds(step * rows, rows)
        parts.append((dq_in.at[part, :], dq_mid.at[part, :], dq_out.at[part, :]))
    fetches = [pltpu.make_async_copy(a, b, sems.at[0, i]) for i, (a, b, _) in enumerate(parts)]
    stores = [pltpu.make_async_copy(b, c, sems.at[1, i]) for i, (_, b, c) in enumerate(parts)]
    for fetch in fetches:
        fetch.start()
    for fetch, store in zip(fetches, stores):
        fetch.wait()
        store.start()
    for store in stores:
        store.wait()


def local(ctx_size, kv_size, queries, key_heads, value_head_rows, out_grad, doc_start):
    block, heads, width = queries.shape
    rows = block * heads
    tiles = rows // TILE
    scale = 1.0 / math.sqrt(width)
    doc = jnp.repeat(doc_start, heads).reshape(-1, 128)
    vmem = pl.BlockSpec(memory_space=pltpu.VMEM)
    stat = (tiles, SPAN * (block // SUB), TILE)
    results = pl.pallas_call(
        functools.partial(kernel, ctx_size, kv_size, block, heads, scale),
        out_shape=[
            jax.ShapeDtypeStruct((rows, width), BF16),
            jax.ShapeDtypeStruct((block, width), BF16),
            jax.ShapeDtypeStruct((block, width), BF16),
        ],
        in_specs=[pl.BlockSpec(memory_space=pl.ANY)] * 5,
        out_specs=[pl.BlockSpec(memory_space=pl.ANY), vmem, vmem],
        scratch_shapes=[
            pltpu.VMEM((rows, width), BF16),
            pltpu.VMEM((block, width), BF16),
            pltpu.VMEM((block, width), BF16),
            pltpu.VMEM((rows, width), BF16),
            pltpu.VMEM((rows, width), BF16),
            pltpu.VMEM((block, TILE), F32),
            pltpu.VMEM((block, TILE), F32),
            pltpu.VMEM((block, TILE), BF16),
            pltpu.VMEM((block, TILE), BF16),
            pltpu.VMEM((SPAN - 1, block, width), BF16),
            pltpu.VMEM((SPAN - 1, block, width), BF16),
            pltpu.VMEM((kv_size,) + doc.shape, jnp.int32),
            pltpu.VMEM((tiles, 1, TILE), jnp.int32),
            pltpu.VMEM((SPAN, tiles, block, TILE), BF16),
            pltpu.VMEM((SPAN, tiles, block, TILE), BF16),
            pltpu.VMEM(stat, F32),
            pltpu.VMEM(stat, F32),
            pltpu.VMEM(stat, F32),
            pltpu.VMEM(stat, F32),
            pltpu.VMEM((tiles, 1, TILE), F32),
            pltpu.VMEM((SPAN, width, block), BF16),
            pltpu.VMEM((tiles, width, TILE), F32),
            pltpu.VMEM((block, width), F32),
            pltpu.VMEM((block, width), F32),
            pltpu.VMEM((SPAN - 1, block, width), BF16),
            pltpu.VMEM((SPAN - 1, block, width), BF16),
            pltpu.VMEM((SPAN - 1, block, width), BF16),
            pltpu.VMEM((SPAN - 1, block, width), BF16),
        ]
        + [pltpu.SemaphoreType.DMA((SPAN - 1,))] * 4
        + [pltpu.SemaphoreType.DMA((kv_size - 1,))] * 2
        + [pltpu.SemaphoreType.DMA((SPAN - 1,))] * 4
        + [pltpu.SemaphoreType.DMA((5,)), pltpu.SemaphoreType.DMA((tiles,))],
        compiler_params=pltpu.CompilerParams(
            collective_id=0, has_side_effects=True, vmem_limit_bytes=56 * 1024 * 1024
        ),
        cost_estimate=pl.CostEstimate(
            flops=10 * rows * SPAN * block * width,
            bytes_accessed=8 * rows * width,
            transcendentals=rows * SPAN * block,
        ),
        name="attention_backward",
    )(
        queries.reshape(rows, width),
        key_heads.reshape(block, width),
        value_head_rows.reshape(block, width),
        out_grad.reshape(rows, width),
        doc,
    )
    anywhere = pl.BlockSpec(memory_space=pl.ANY)
    query_grad, key_grad, value_grad = pl.pallas_call(
        hand_over,
        out_shape=[jax.ShapeDtypeStruct(x.shape, x.dtype) for x in results],
        in_specs=[anywhere] * 3,
        out_specs=[anywhere] * 3,
        scratch_shapes=[pltpu.VMEM(x.shape, x.dtype) for x in results]
        + [pltpu.SemaphoreType.DMA((2, STEPS + 2))],
        name="hand_over",
    )(*results)
    return (
        query_grad.reshape(queries.shape),
        key_grad.reshape(key_heads.shape),
        value_grad.reshape(value_head_rows.shape),
    )


def solution(mesh):
    return jax.shard_map(
        functools.partial(local, mesh.shape["ctx"], mesh.shape["kv"]),
        mesh=mesh,
        in_specs=(
            P("ctx", "kv", None),
            P("ctx", "kv", None),
            P("ctx", "kv", None),
            P("ctx", "kv", None),
            P(("ctx", "kv")),
        ),
        out_specs=(P("ctx", "kv", None), P("ctx", "kv", None), P("ctx", "kv", None)),
        check_vma=False,
    )
```

```python
import functools
import math

import jax
import jax.numpy as jnp
from jax import lax
from jax.experimental import pallas as pl
from jax.experimental.pallas import tpu as pltpu
from jax.sharding import PartitionSpec as P

SPAN = 4
FILL = -1e30
TILE = 512
SUB = 256
CUT = 128
LANES = 128
STEPS = 4
MESH = pl.DeviceIdType.MESH
F32 = jnp.float32
BF16 = jnp.bfloat16


def dot(a, b, dims):
    return lax.dot_general(a, b, (dims, ((), ())), preferred_element_type=F32)


def kernel(
    ctx_size, kv_size, block, per_group, scale,
    q_any, k_any, v_any, do_any, doc_any,
    dq_any, dk_ref, dv_ref,
    q_ref, k_ref, v_ref, do_ref, dq_ref,
    kbuf, vbuf, docbuf, lower, probs, dprobs, top, total, rowdot, weight, shift,
    ktrans, dq_acc, dk_acc, dv_acc, dk_out, dv_out, dk_in, dv_in,
    send_k, recv_k, send_v, recv_v, send_d, recv_d, send_gk, recv_gk, send_gv, recv_gv,
    load_sem, store_sem,
):
    tiles = q_ref.shape[0] // TILE
    toks = TILE // per_group
    subs = block // SUB
    base2 = scale * math.log2(math.e)
    ctx = lax.axis_index("ctx")
    kv = lax.axis_index("kv")
    odd = lax.rem(ctx, 2)

    def ahead(steps):
        return {"ctx": lax.rem(ctx + steps + ctx_size, ctx_size)}

    def beside(steps):
        return {"kv": lax.rem(kv + steps, kv_size)}

    loads = [
        pltpu.make_async_copy(src, dst, load_sem.at[i])
        for i, (src, dst) in enumerate(
            (
                (doc_any, docbuf.at[kv]), (k_any, k_ref), (q_any, q_ref),
                (v_any, v_ref), (do_any, do_ref),
            )
        )
    ]
    for copy in loads:
        copy.start()

    partner = {"ctx": ctx + 1 - 2 * odd}

    barrier = pltpu.get_barrier_semaphore()
    for steps in (1, -1, 3, -3):
        pl.semaphore_signal(barrier, inc=1, device_id=ahead(steps), device_id_type=MESH)
    for steps in range(1, kv_size):
        pl.semaphore_signal(barrier, inc=1, device_id=beside(steps), device_id_type=MESH)
    pl.semaphore_wait(barrier, 4 + kv_size - 1)

    doc_copies = []
    for steps in range(1, kv_size):
        doc_copies.append(
            pltpu.make_async_remote_copy(
                src_ref=doc_any, dst_ref=docbuf.at[kv],
                send_sem=send_d.at[steps - 1], recv_sem=recv_d.at[steps - 1],
                device_id=beside(steps), device_id_type=MESH,
            )
        )
        doc_copies[-1].start()

    def both(sources, targets, slot, sends, recvs, device):
        return [
            pltpu.make_async_remote_copy(
                src_ref=src, dst_ref=dst.at[slot],
                send_sem=send.at[slot], recv_sem=recv.at[slot],
                device_id=device, device_id_type=MESH,
            )
            for src, dst, send, recv in zip(sources, targets, sends, recvs)
        ]

    def start(copies):
        for copy in copies:
            copy.start()

    def received(copies):
        for copy in copies:
            copy.wait_recv()

    kv_buffers = ((kbuf, vbuf), (send_k, send_v), (recv_k, recv_v))
    one, three = [
        both((k_any, v_any), kv_buffers[0], steps - 1, kv_buffers[1], kv_buffers[2], ahead(steps))
        for steps in (1, 3)
    ]
    start(one)
    start(three)
    passed_on = both(
        (kbuf.at[2 * odd], vbuf.at[2 * odd]), kv_buffers[0], 1, kv_buffers[1], kv_buffers[2], partner
    )

    for copy in loads:
        copy.wait()
    ktrans[0] = k_ref[...].T
    top[...] = jnp.full_like(top, FILL)
    total[...] = jnp.zeros_like(total)
    rowdot[...] = jnp.zeros_like(rowdot)
    for copy in doc_copies:
        copy.wait()
    per_dev = docbuf.shape[1]
    for tile in range(tiles):
        parts = []
        for piece in range(TILE // 128):
            row = tile * (TILE // 128) + piece
            parts.append(docbuf[row // per_dev, pl.ds(row % per_dev, 1), :])
        lower[tile] = jnp.concatenate(parts, axis=1) - ctx * block

    def rows_of(tile):
        return pl.ds(pl.multiple_of(tile * TILE, TILE), TILE)

    def pieces(key_count):
        return [(start, min(SUB, key_count - start)) for start in range(0, key_count, SUB)]

    def forward(offset, keys, values, key_count, tile):
        rows = rows_of(tile)
        raw = dot(keys[pl.ds(0, key_count), :], q_ref[rows, :], ((1,), (1,)))
        gradient = dot(values[pl.ds(0, key_count), :], do_ref[rows, :], ((1,), (1,)))
        first = lower[tile] + offset * block
        lane_token = lax.broadcasted_iota(jnp.int32, (1, LANES), 1) // per_group
        for lane in range(0, TILE, LANES):
            lanes = slice(lane, lane + LANES)
            for start, size in pieces(key_count):
                position = lax.broadcasted_iota(jnp.int32, (size, LANES), 0)
                part = slice(start, start + size)
                allowed = position >= first[:, lanes] - start
                if offset == 0:
                    token = lane_token + (tile * toks + lane // per_group - start)
                    allowed = allowed & (position <= token)
                scores = jnp.where(allowed, raw[part, lanes], FILL).reshape(size // 8, 8, LANES)
                chunk = gradient[part, lanes]
                highest = jnp.max(scores, axis=0)
                unscaled = jnp.exp2((scores - highest[None]) * base2)
                line = pl.ds((offset * subs + start // SUB) * 8, 8)
                top[tile, line, lanes] = highest
                total[tile, line, lanes] = jnp.sum(unscaled, axis=0)
                rowdot[tile, line, lanes] = jnp.sum(unscaled * chunk.reshape(scores.shape), axis=0)
                probs[offset, tile, pl.ds(start, size), lanes] = unscaled.reshape(size, LANES).astype(BF16)
                dprobs[offset, tile, pl.ds(start, size), lanes] = chunk.astype(BF16)

    def backward(offset, first, keys, key_count, tile):
        rows = rows_of(tile)
        r = shift[tile]
        prob_parts = []
        score_parts = []
        for start, size in pieces(key_count):
            part = pl.ds(start, size)
            repeats = size // 16
            w = weight[tile, pl.ds((offset * subs + start // SUB) * 16, 16), :]
            prob_parts.append(probs[offset, tile, part, :] * jnp.concatenate([w] * repeats, axis=0))
            score_parts.append(
                prob_parts[-1] * (dprobs[offset, tile, part, :] - jnp.concatenate([r] * repeats, axis=0))
            )
        prob = jnp.concatenate(prob_parts, axis=0)
        score = jnp.concatenate(score_parts, axis=0)
        dv_acc[pl.ds(0, key_count), :] += dot(prob, do_ref[rows, :], ((1,), (0,)))
        dk_acc[pl.ds(0, key_count), :] += dot(score, q_ref[rows, :], ((1,), (0,)))
        part = dot(ktrans[offset, :, pl.ds(0, key_count)], score, ((1,), (0,)))
        if first:
            dq_acc[tile] = part
        elif offset > 0:
            dq_acc[tile] += part
        else:
            dq_ref[rows, :] = ((dq_acc[tile] + part) * scale).T.astype(BF16)
            stores[tile].start()

    stores = [
        pltpu.make_async_copy(
            dq_ref.at[pl.ds(tile * TILE, TILE), :], dq_any.at[pl.ds(tile * TILE, TILE), :], store_sem.at[tile]
        )
        for tile in range(tiles)
    ]

    def over(body):
        def step(pair, carry):
            body(2 * pair)
            body(2 * pair + 1)
            return carry

        lax.fori_loop(0, tiles // 2, step, 0)

    def over_own(body):
        for tile in range(tiles):
            body(CUT * (((tile + 1) * toks + CUT - 1) // CUT), tile)

    def visit(offset):
        ktrans[offset] = kbuf[offset - 1].T
        over(functools.partial(forward, offset, kbuf.at[offset - 1], vbuf.at[offset - 1], block))

    over_own(functools.partial(forward, 0, k_ref, v_ref))
    received(one)

    @pl.when(odd == 0)
    def _():
        start(passed_on)

    visit(1)
    received(three)

    @pl.when(odd == 1)
    def _():
        start(passed_on)

    visit(3)
    received(passed_on)
    visit(2)

    def combine(tile):
        tops = top[tile]
        factors = jnp.exp2((tops - jnp.max(tops, axis=0, keepdims=True)) * base2)
        inverse = 1.0 / jnp.sum(factors * total[tile], axis=0, keepdims=True)
        dotted = jnp.sum(factors * rowdot[tile], axis=0, keepdims=True) * inverse
        shift[tile] = jnp.broadcast_to(dotted, (16, TILE)).astype(BF16)
        scaled = factors * inverse
        for group in range(SPAN * subs):
            half = scaled[group * 8 : group * 8 + 8]
            weight[tile, pl.ds(group * 16, 16), :] = jnp.concatenate([half, half], axis=0).astype(BF16)

    over(combine)

    def accumulate(offset, first):
        dk_acc[...] = jnp.zeros_like(dk_acc)
        dv_acc[...] = jnp.zeros_like(dv_acc)
        over(functools.partial(backward, offset, first, kbuf.at[offset - 1], block))
        dk_acc[...] = dk_acc[...] * scale

    grad_sends, grad_recvs = (send_gk, send_gv), (recv_gk, recv_gv)

    def give(offset, device):
        slot = offset - 1
        dk_out[slot] = dk_acc[...].astype(BF16)
        dv_out[slot] = dv_acc[...].astype(BF16)
        copies = both(
            (dk_out.at[slot], dv_out.at[slot]), (dk_in, dv_in), slot, grad_sends, grad_recvs, device
        )
        start(copies)
        return copies

    def take(slot):
        dk_acc[...] += dk_in[slot].astype(F32)
        dv_acc[...] += dv_in[slot].astype(F32)

    accumulate(2, True)
    given_two = give(2, partner)
    accumulate(3, False)

    @pl.when(odd == 1)
    def _():
        received(given_two)
        take(1)

    given_three = give(3, ahead(-3))
    accumulate(1, False)

    @pl.when(odd == 0)
    def _():
        received(given_two)
        take(1)

    given_one = give(1, ahead(-1))
    dk_acc[...] = jnp.zeros_like(dk_acc)
    dv_acc[...] = jnp.zeros_like(dv_acc)
    over_own(functools.partial(backward, 0, False, k_ref))
    dk_acc[...] = dk_acc[...] * scale
    received(given_three)
    take(2)
    received(given_one)
    take(0)
    dv_ref[...] = dv_acc[...].astype(BF16)
    dk_ref[...] = dk_acc[...].astype(BF16)
    for copies in (one, three, passed_on, given_two, given_three, given_one):
        for copy in copies:
            copy.wait_send()
    for copy in stores:
        copy.wait()


def hand_over(dq_in, dk_in, dv_in, dq_out, dk_out, dv_out, dq_mid, dk_mid, dv_mid, sems):
    parts = [(dk_in, dk_mid, dk_out), (dv_in, dv_mid, dv_out)]
    rows = dq_in.shape[0] // STEPS
    for step in range(STEPS):
        part = pl.ds(step * rows, rows)
        parts.append((dq_in.at[part, :], dq_mid.at[part, :], dq_out.at[part, :]))
    fetches = [pltpu.make_async_copy(a, b, sems.at[0, i]) for i, (a, b, _) in enumerate(parts)]
    stores = [pltpu.make_async_copy(b, c, sems.at[1, i]) for i, (_, b, c) in enumerate(parts)]
    for fetch in fetches:
        fetch.start()
    for fetch, store in zip(fetches, stores):
        fetch.wait()
        store.start()
    for store in stores:
        store.wait()


def local(ctx_size, kv_size, queries, key_heads, value_head_rows, out_grad, doc_start):
    block, heads, width = queries.shape
    rows = block * heads
    tiles = rows // TILE
    scale = 1.0 / math.sqrt(width)
    doc = jnp.repeat(doc_start, heads).reshape(-1, 128)
    vmem = pl.BlockSpec(memory_space=pltpu.VMEM)
    stat = (tiles, SPAN * (block // SUB) * 8, TILE)
    results = pl.pallas_call(
        functools.partial(kernel, ctx_size, kv_size, block, heads, scale),
        out_shape=[
            jax.ShapeDtypeStruct((rows, width), BF16),
            jax.ShapeDtypeStruct((block, width), BF16),
            jax.ShapeDtypeStruct((block, width), BF16),
        ],
        in_specs=[pl.BlockSpec(memory_space=pl.ANY)] * 5,
        out_specs=[pl.BlockSpec(memory_space=pl.ANY), vmem, vmem],
        scratch_shapes=[
            pltpu.VMEM((rows, width), BF16),
            pltpu.VMEM((block, width), BF16),
            pltpu.VMEM((block, width), BF16),
            pltpu.VMEM((rows, width), BF16),
            pltpu.VMEM((rows, width), BF16),
            pltpu.VMEM((SPAN - 1, block, width), BF16),
            pltpu.VMEM((SPAN - 1, block, width), BF16),
            pltpu.VMEM((kv_size,) + doc.shape, jnp.int32),
            pltpu.VMEM((tiles, 1, TILE), jnp.int32),
            pltpu.VMEM((SPAN, tiles, block, TILE), BF16),
            pltpu.VMEM((SPAN, tiles, block, TILE), BF16),
            pltpu.VMEM(stat, F32),
            pltpu.VMEM(stat, F32),
            pltpu.VMEM(stat, F32),
            pltpu.VMEM((tiles, 2 * stat[1], TILE), BF16),
            pltpu.VMEM((tiles, 16, TILE), BF16),
            pltpu.VMEM((SPAN, width, block), BF16),
            pltpu.VMEM((tiles, width, TILE), F32),
            pltpu.VMEM((block, width), F32),
            pltpu.VMEM((block, width), F32),
            pltpu.VMEM((SPAN - 1, block, width), BF16),
            pltpu.VMEM((SPAN - 1, block, width), BF16),
            pltpu.VMEM((SPAN - 1, block, width), BF16),
            pltpu.VMEM((SPAN - 1, block, width), BF16),
        ]
        + [pltpu.SemaphoreType.DMA((SPAN - 1,))] * 4
        + [pltpu.SemaphoreType.DMA((kv_size - 1,))] * 2
        + [pltpu.SemaphoreType.DMA((SPAN - 1,))] * 4
        + [pltpu.SemaphoreType.DMA((5,)), pltpu.SemaphoreType.DMA((tiles,))],
        compiler_params=pltpu.CompilerParams(
            collective_id=0, has_side_effects=True, vmem_limit_bytes=56 * 1024 * 1024
        ),
        cost_estimate=pl.CostEstimate(
            flops=10 * rows * SPAN * block * width,
            bytes_accessed=8 * rows * width,
            transcendentals=rows * SPAN * block,
        ),
        name="attention_backward",
    )(
        queries.reshape(rows, width),
        key_heads.reshape(block, width),
        value_head_rows.reshape(block, width),
        out_grad.reshape(rows, width),
        doc,
    )
    anywhere = pl.BlockSpec(memory_space=pl.ANY)
    query_grad, key_grad, value_grad = pl.pallas_call(
        hand_over,
        out_shape=[jax.ShapeDtypeStruct(x.shape, x.dtype) for x in results],
        in_specs=[anywhere] * 3,
        out_specs=[anywhere] * 3,
        scratch_shapes=[pltpu.VMEM(x.shape, x.dtype) for x in results]
        + [pltpu.SemaphoreType.DMA((2, STEPS + 2))],
        name="hand_over",
    )(*results)
    return (
        query_grad.reshape(queries.shape),
        key_grad.reshape(key_heads.shape),
        value_grad.reshape(value_head_rows.shape),
    )


def solution(mesh):
    return jax.shard_map(
        functools.partial(local, mesh.shape["ctx"], mesh.shape["kv"]),
        mesh=mesh,
        in_specs=(
            P("ctx", "kv", None),
            P("ctx", "kv", None),
            P("ctx", "kv", None),
            P("ctx", "kv", None),
            P(("ctx", "kv")),
        ),
        out_specs=(P("ctx", "kv", None), P("ctx", "kv", None), P("ctx", "kv", None)),
        check_vma=False,
    )
```

```python
import functools
import math

import jax
import jax.numpy as jnp
from jax import lax
from jax.experimental import pallas as pl
from jax.experimental.pallas import tpu as pltpu
from jax.sharding import PartitionSpec as P

SPAN = 4
FILL = -1e30
TILE = 512
SUB = 256
CUT = 128
LANES = 128
STEPS = 4
MESH = pl.DeviceIdType.MESH
F32 = jnp.float32
BF16 = jnp.bfloat16


def dot(a, b, dims):
    return lax.dot_general(a, b, (dims, ((), ())), preferred_element_type=F32)


def kernel(
    ctx_size, kv_size, block, per_group, scale,
    q_any, k_any, v_any, do_any, doc_any,
    dq_any, dk_ref, dv_ref,
    q_ref, k_ref, v_ref, do_ref, dq_ref,
    kbuf, vbuf, docbuf, lower, probs, dprobs, top, total, rowdot, weight, shift,
    ktrans, dq_acc, dk_acc, dv_acc, dk_out, dv_out, dk_in, dv_in,
    send_k, recv_k, send_v, recv_v, send_d, recv_d, send_gk, recv_gk, send_gv, recv_gv,
    load_sem, store_sem,
):
    tiles = q_ref.shape[0] // TILE
    toks = TILE // per_group
    subs = block // SUB
    base2 = scale * math.log2(math.e)
    ctx = lax.axis_index("ctx")
    kv = lax.axis_index("kv")
    odd = lax.rem(ctx, 2)

    def ahead(steps):
        return {"ctx": lax.rem(ctx + steps + ctx_size, ctx_size)}

    def beside(steps):
        return {"kv": lax.rem(kv + steps, kv_size)}

    loads = [
        pltpu.make_async_copy(src, dst, load_sem.at[i])
        for i, (src, dst) in enumerate(
            (
                (doc_any, docbuf.at[kv]), (k_any, k_ref), (q_any, q_ref),
                (v_any, v_ref), (do_any, do_ref),
            )
        )
    ]
    for copy in loads:
        copy.start()

    partner = {"ctx": ctx + 1 - 2 * odd}

    barrier = pltpu.get_barrier_semaphore()
    for steps in (1, -1, 3, -3):
        pl.semaphore_signal(barrier, inc=1, device_id=ahead(steps), device_id_type=MESH)
    for steps in range(1, kv_size):
        pl.semaphore_signal(barrier, inc=1, device_id=beside(steps), device_id_type=MESH)
    pl.semaphore_wait(barrier, 4 + kv_size - 1)

    doc_copies = []
    for steps in range(1, kv_size):
        doc_copies.append(
            pltpu.make_async_remote_copy(
                src_ref=doc_any, dst_ref=docbuf.at[kv],
                send_sem=send_d.at[steps - 1], recv_sem=recv_d.at[steps - 1],
                device_id=beside(steps), device_id_type=MESH,
            )
        )
        doc_copies[-1].start()

    def both(sources, targets, slot, sends, recvs, device):
        return [
            pltpu.make_async_remote_copy(
                src_ref=src, dst_ref=dst.at[slot],
                send_sem=send.at[slot], recv_sem=recv.at[slot],
                device_id=device, device_id_type=MESH,
            )
            for src, dst, send, recv in zip(sources, targets, sends, recvs)
        ]

    def start(copies):
        for copy in copies:
            copy.start()

    def received(copies):
        for copy in copies:
            copy.wait_recv()

    kv_buffers = ((kbuf, vbuf), (send_k, send_v), (recv_k, recv_v))
    one, three = [
        both((k_any, v_any), kv_buffers[0], steps - 1, kv_buffers[1], kv_buffers[2], ahead(steps))
        for steps in (1, 3)
    ]
    start(one)
    start(three)
    passed_on = both(
        (kbuf.at[2 * odd], vbuf.at[2 * odd]), kv_buffers[0], 1, kv_buffers[1], kv_buffers[2], partner
    )

    for copy in loads:
        copy.wait()
    ktrans[0] = k_ref[...].T
    top[...] = jnp.full_like(top, FILL)
    total[...] = jnp.zeros_like(total)
    rowdot[...] = jnp.zeros_like(rowdot)
    for copy in doc_copies:
        copy.wait()
    per_dev = docbuf.shape[1]
    for tile in range(tiles):
        parts = []
        for piece in range(TILE // 128):
            row = tile * (TILE // 128) + piece
            parts.append(docbuf[row // per_dev, pl.ds(row % per_dev, 1), :])
        lower[tile] = jnp.concatenate(parts, axis=1) - ctx * block

    def rows_of(tile):
        return pl.ds(pl.multiple_of(tile * TILE, TILE), TILE)

    def pieces(key_count):
        return [(start, min(SUB, key_count - start)) for start in range(0, key_count, SUB)]

    def forward(offset, keys, values, key_count, tile):
        rows = rows_of(tile)
        raw = dot(keys[pl.ds(0, key_count), :], q_ref[rows, :], ((1,), (1,)))
        gradient = dot(values[pl.ds(0, key_count), :], do_ref[rows, :], ((1,), (1,)))
        first = lower[tile] + offset * block
        lane_token = lax.broadcasted_iota(jnp.int32, (1, LANES), 1) // per_group
        for lane in range(0, TILE, LANES):
            lanes = slice(lane, lane + LANES)
            for start, size in pieces(key_count):
                position = lax.broadcasted_iota(jnp.int32, (size, LANES), 0)
                part = slice(start, start + size)
                allowed = position >= first[:, lanes] - start
                if offset == 0:
                    token = lane_token + (tile * toks + lane // per_group - start)
                    allowed = allowed & (position <= token)
                scores = jnp.where(allowed, raw[part, lanes], FILL).reshape(size // 8, 8, LANES)
                chunk = gradient[part, lanes]
                highest = jnp.max(scores, axis=0)
                unscaled = jnp.exp2((scores - highest[None]) * base2)
                line = pl.ds((offset * subs + start // SUB) * 8, 8)
                top[tile, line, lanes] = highest
                total[tile, line, lanes] = jnp.sum(unscaled, axis=0)
                rowdot[tile, line, lanes] = jnp.sum(unscaled * chunk.reshape(scores.shape), axis=0)
                probs[offset, tile, pl.ds(start, size), lanes] = unscaled.reshape(size, LANES).astype(BF16)
                dprobs[offset, tile, pl.ds(start, size), lanes] = chunk.astype(BF16)

    def backward(offset, first, keys, key_count, tile):
        rows = pl.ds(pl.multiple_of(tile * TILE, 2 * TILE), 2 * TILE)
        probs_of, scores_of = [], []
        for now in (tile, tile + 1):
            r = shift[now]
            prob_parts, score_parts = [], []
            for start, size in pieces(key_count):
                part = pl.ds(start, size)
                repeats = size // 16
                w = weight[now, pl.ds((offset * subs + start // SUB) * 16, 16), :]
                prob_parts.append(probs[offset, now, part, :] * jnp.concatenate([w] * repeats, axis=0))
                score_parts.append(
                    prob_parts[-1] * (dprobs[offset, now, part, :] - jnp.concatenate([r] * repeats, axis=0))
                )
            probs_of.append(jnp.concatenate(prob_parts, axis=0))
            scores_of.append(jnp.concatenate(score_parts, axis=0))
        score = jnp.concatenate(scores_of, axis=1)
        count = pl.ds(0, key_count)
        dv_acc[count, :] += dot(jnp.concatenate(probs_of, axis=1), do_ref[rows, :], ((1,), (0,)))
        dk_acc[count, :] += dot(score, q_ref[rows, :], ((1,), (0,)))
        part = dot(ktrans[offset, :, count], score, ((1,), (0,)))
        pair = tile // 2
        if first:
            dq_acc[pair] = part
        elif offset > 0:
            dq_acc[pair] += part
        else:
            dq_ref[rows, :] = ((dq_acc[pair] + part) * scale).T.astype(BF16)
            stores[pair].start()

    pair_rows = [pl.ds(start, 2 * TILE) for start in range(0, tiles * TILE, 2 * TILE)]
    stores = [
        pltpu.make_async_copy(dq_ref.at[part, :], dq_any.at[part, :], store_sem.at[pair])
        for pair, part in enumerate(pair_rows)
    ]

    def over(body, stride=1):
        def step(index, carry):
            for part in range(0, 4, stride):
                body(4 * index + part)
            return carry

        lax.fori_loop(0, tiles // 4, step, 0)

    def over_own(body, stride=1):
        for tile in range(0, tiles, stride):
            body(CUT * (((tile + stride) * toks + CUT - 1) // CUT), tile)

    def visit(offset):
        ktrans[offset] = kbuf[offset - 1].T
        over(functools.partial(forward, offset, kbuf.at[offset - 1], vbuf.at[offset - 1], block))

    over_own(functools.partial(forward, 0, k_ref, v_ref))
    received(one)

    @pl.when(odd == 0)
    def _():
        start(passed_on)

    visit(1)
    received(three)

    @pl.when(odd == 1)
    def _():
        start(passed_on)

    visit(3)
    received(passed_on)
    visit(2)

    def combine(tile):
        tops = top[tile]
        factors = jnp.exp2((tops - jnp.max(tops, axis=0, keepdims=True)) * base2)
        inverse = 1.0 / jnp.sum(factors * total[tile], axis=0, keepdims=True)
        dotted = jnp.sum(factors * rowdot[tile], axis=0, keepdims=True) * inverse
        shift[tile] = jnp.broadcast_to(dotted, (16, TILE)).astype(BF16)
        scaled = factors * inverse
        for group in range(SPAN * subs):
            half = scaled[group * 8 : group * 8 + 8]
            weight[tile, pl.ds(group * 16, 16), :] = jnp.concatenate([half, half], axis=0).astype(BF16)

    over(combine)

    def accumulate(offset, first):
        dk_acc[...] = jnp.zeros_like(dk_acc)
        dv_acc[...] = jnp.zeros_like(dv_acc)
        over(functools.partial(backward, offset, first, kbuf.at[offset - 1], block), 2)
        dk_acc[...] = dk_acc[...] * scale

    grad_sends, grad_recvs = (send_gk, send_gv), (recv_gk, recv_gv)

    def give(offset, device):
        slot = offset - 1
        dk_out[slot] = dk_acc[...].astype(BF16)
        dv_out[slot] = dv_acc[...].astype(BF16)
        copies = both(
            (dk_out.at[slot], dv_out.at[slot]), (dk_in, dv_in), slot, grad_sends, grad_recvs, device
        )
        start(copies)
        return copies

    def take(slot):
        dk_acc[...] += dk_in[slot].astype(F32)
        dv_acc[...] += dv_in[slot].astype(F32)

    accumulate(2, True)
    given_two = give(2, partner)
    accumulate(3, False)

    @pl.when(odd == 1)
    def _():
        received(given_two)
        take(1)

    given_three = give(3, ahead(-3))
    accumulate(1, False)

    @pl.when(odd == 0)
    def _():
        received(given_two)
        take(1)

    given_one = give(1, ahead(-1))
    dk_acc[...] = jnp.zeros_like(dk_acc)
    dv_acc[...] = jnp.zeros_like(dv_acc)
    over_own(functools.partial(backward, 0, False, k_ref), 2)
    dk_acc[...] = dk_acc[...] * scale
    received(given_three)
    take(2)
    received(given_one)
    take(0)
    dv_ref[...] = dv_acc[...].astype(BF16)
    dk_ref[...] = dk_acc[...].astype(BF16)
    for copies in (one, three, passed_on, given_two, given_three, given_one):
        for copy in copies:
            copy.wait_send()
    for copy in stores:
        copy.wait()


def hand_over(dq_in, dk_in, dv_in, dq_out, dk_out, dv_out, dq_mid, dk_mid, dv_mid, sems):
    parts = [(dk_in, dk_mid, dk_out), (dv_in, dv_mid, dv_out)]
    rows = dq_in.shape[0] // STEPS
    for step in range(STEPS):
        part = pl.ds(step * rows, rows)
        parts.append((dq_in.at[part, :], dq_mid.at[part, :], dq_out.at[part, :]))
    fetches = [pltpu.make_async_copy(a, b, sems.at[0, i]) for i, (a, b, _) in enumerate(parts)]
    stores = [pltpu.make_async_copy(b, c, sems.at[1, i]) for i, (_, b, c) in enumerate(parts)]
    for fetch in fetches:
        fetch.start()
    for fetch, store in zip(fetches, stores):
        fetch.wait()
        store.start()
    for store in stores:
        store.wait()


def local(ctx_size, kv_size, queries, key_heads, value_head_rows, out_grad, doc_start):
    block, heads, width = queries.shape
    rows = block * heads
    tiles = rows // TILE
    scale = 1.0 / math.sqrt(width)
    doc = jnp.repeat(doc_start, heads).reshape(-1, 128)
    vmem = pl.BlockSpec(memory_space=pltpu.VMEM)
    stat = (tiles, SPAN * (block // SUB) * 8, TILE)
    results = pl.pallas_call(
        functools.partial(kernel, ctx_size, kv_size, block, heads, scale),
        out_shape=[
            jax.ShapeDtypeStruct((rows, width), BF16),
            jax.ShapeDtypeStruct((block, width), BF16),
            jax.ShapeDtypeStruct((block, width), BF16),
        ],
        in_specs=[pl.BlockSpec(memory_space=pl.ANY)] * 5,
        out_specs=[pl.BlockSpec(memory_space=pl.ANY), vmem, vmem],
        scratch_shapes=[
            pltpu.VMEM((rows, width), BF16),
            pltpu.VMEM((block, width), BF16),
            pltpu.VMEM((block, width), BF16),
            pltpu.VMEM((rows, width), BF16),
            pltpu.VMEM((rows, width), BF16),
            pltpu.VMEM((SPAN - 1, block, width), BF16),
            pltpu.VMEM((SPAN - 1, block, width), BF16),
            pltpu.VMEM((kv_size,) + doc.shape, jnp.int32),
            pltpu.VMEM((tiles, 1, TILE), jnp.int32),
            pltpu.VMEM((SPAN, tiles, block, TILE), BF16),
            pltpu.VMEM((SPAN, tiles, block, TILE), BF16),
            pltpu.VMEM(stat, F32),
            pltpu.VMEM(stat, F32),
            pltpu.VMEM(stat, F32),
            pltpu.VMEM((tiles, 2 * stat[1], TILE), BF16),
            pltpu.VMEM((tiles, 16, TILE), BF16),
            pltpu.VMEM((SPAN, width, block), BF16),
            pltpu.VMEM((tiles // 2, width, 2 * TILE), F32),
            pltpu.VMEM((block, width), F32),
            pltpu.VMEM((block, width), F32),
            pltpu.VMEM((SPAN - 1, block, width), BF16),
            pltpu.VMEM((SPAN - 1, block, width), BF16),
            pltpu.VMEM((SPAN - 1, block, width), BF16),
            pltpu.VMEM((SPAN - 1, block, width), BF16),
        ]
        + [pltpu.SemaphoreType.DMA((SPAN - 1,))] * 4
        + [pltpu.SemaphoreType.DMA((kv_size - 1,))] * 2
        + [pltpu.SemaphoreType.DMA((SPAN - 1,))] * 4
        + [pltpu.SemaphoreType.DMA((5,)), pltpu.SemaphoreType.DMA((tiles // 2,))],
        compiler_params=pltpu.CompilerParams(
            collective_id=0, has_side_effects=True, vmem_limit_bytes=56 * 1024 * 1024
        ),
        cost_estimate=pl.CostEstimate(
            flops=10 * rows * SPAN * block * width,
            bytes_accessed=8 * rows * width,
            transcendentals=rows * SPAN * block,
        ),
        name="attention_backward",
    )(
        queries.reshape(rows, width),
        key_heads.reshape(block, width),
        value_head_rows.reshape(block, width),
        out_grad.reshape(rows, width),
        doc,
    )
    anywhere = pl.BlockSpec(memory_space=pl.ANY)
    query_grad, key_grad, value_grad = pl.pallas_call(
        hand_over,
        out_shape=[jax.ShapeDtypeStruct(x.shape, x.dtype) for x in results],
        in_specs=[anywhere] * 3,
        out_specs=[anywhere] * 3,
        scratch_shapes=[pltpu.VMEM(x.shape, x.dtype) for x in results]
        + [pltpu.SemaphoreType.DMA((2, STEPS + 2))],
        name="hand_over",
    )(*results)
    return (
        query_grad.reshape(queries.shape),
        key_grad.reshape(key_heads.shape),
        value_grad.reshape(value_head_rows.shape),
    )


def solution(mesh):
    return jax.shard_map(
        functools.partial(local, mesh.shape["ctx"], mesh.shape["kv"]),
        mesh=mesh,
        in_specs=(
            P("ctx", "kv", None),
            P("ctx", "kv", None),
            P("ctx", "kv", None),
            P("ctx", "kv", None),
            P(("ctx", "kv")),
        ),
        out_specs=(P("ctx", "kv", None), P("ctx", "kv", None), P("ctx", "kv", None)),
        check_vma=False,
    )
```
